32 devices in a mesh: ctx: 8 (over z, y), head: 4 (over x, core).
Axes of the slice: x: 2, y: 2, z: 4, core: 2. Of those that a mesh axis runs over, the one named last changes fastest.
Arguments:
- queries: bfloat16 [8192, 4096], P('ctx', 'head'), as said below
- key_value: bfloat16 [2, 8192, 4096], P(None, 'ctx', 'head'), as said below
- lanczos_vec: float32 [8192, 4096], P('ctx', 'head'), as said below
- rand_blocks: int32 [64, 3], replicated, may hold values from 0 to 63, as said below
- global_ids: int32 [2], replicated, may hold values from 0 to 63
Outputs:
- next_vec: float32 [8192, 4096], P('ctx', 'head')
- coefficients: float32 [2], replicated
The draws below stay inside these ranges and needn't reach their ends.
Inputs may be any that keep to these rules, and one draw needn't show every extreme that they name: `rand_blocks`: row b lists the random key blocks of query block b. For each shard of 8 query blocks along ctx and each shard of 8 key blocks, at most 3 of the shard's listed random blocks lie in that key shard, and every query shard reaches 3 with some key shard. `queries`: entries are of order one or a few tens. `key_value`: keys of order one, values of order one to a few hundred. `lanczos_vec`: nonzero real entries; the mean of their squares over all entries is one, up to float32 rounding.
All inputs are finite; a program needn't handle non-finite values.
Results may differ from the reference program's by a relative error of at most 0.0049.
Values may be sent and summed in bfloat16 or wider, within the bound.
A program may use at most 192 MiB of HBM per device.

```python
import jax
import jax.numpy as jnp
from jax import lax

HEADS = 32
HD = 128
BS = 128
RAND = 3
GLOB = 2
QB_DEV = 8
DM = 4096
NB = 64
SEQ = 8192
N_CTX = 8


def shared_keys(key):
    base = jax.random.truncated_normal(jax.random.fold_in(key, 101), -6.0, 6.0, (SEQ, HEADS * HD), jnp.float32)
    return base


def draw_key_value(key, part):
    keys = shared_keys(key)
    block_factor = 10.0 ** jax.random.uniform(jax.random.fold_in(key, 105), (SEQ // BS,), jnp.float32, 0.0, 1.5)
    row_factor = jnp.repeat(block_factor, BS)
    values = 3.0 * jax.random.truncated_normal(jax.random.fold_in(key, 103), -6.0, 6.0, (SEQ, HEADS * HD), jnp.float32)
    values = values * row_factor[:, None]
    return jnp.stack([keys, values]).astype(jnp.bfloat16)


def draw_queries(key, part):
    base = jax.random.truncated_normal(jax.random.fold_in(key, 104), -6.0, 6.0, (SEQ, HEADS * HD), jnp.float32)
    return base.astype(jnp.bfloat16)


def draw_lanczos_vec(key, part):
    position = jnp.arange(SEQ, dtype=jnp.float32) / SEQ
    row_scale = 10.0 ** jax.random.uniform(jax.random.fold_in(key, 201), (SEQ,), jnp.float32)
    col_scale = 10.0 ** jax.random.uniform(jax.random.fold_in(key, 202), (HEADS * HD,), jnp.float32)
    noise = jax.random.truncated_normal(jax.random.fold_in(key, 204), -4.0, 4.0, (SEQ, HEADS * HD), jnp.float32)
    ramp = 3.0 ** position
    raw = noise * (ramp * row_scale)[:, None] * col_scale[None, :]
    spread = jnp.sqrt(jnp.mean(raw * raw))
    return (raw / spread).astype(jnp.float32)


def draw_rand_blocks(key, part):
    request_count = QB_DEV * RAND
    perm_keys = jax.random.split(jax.random.fold_in(key, 301), N_CTX)
    orders = jax.vmap(lambda single: jax.random.permutation(single, N_CTX))(perm_keys)
    columns = jnp.arange(request_count) % N_CTX
    sources = orders[:, columns]
    inside = jax.random.randint(jax.random.fold_in(key, 302), (N_CTX, request_count), 0, QB_DEV)
    return (sources * QB_DEV + inside).reshape(N_CTX * QB_DEV, RAND).astype(jnp.int32)


def setup_inputs(seed: int = 0) -> dict:
    seeds = jax.random.split(jax.random.key(seed), 6)
    queries = draw_queries(jax.random.fold_in(seeds[5], 71), 0)
    key_value = draw_key_value(jax.random.fold_in(seeds[5], 71), 0)
    lanczos_vec = draw_lanczos_vec(jax.random.fold_in(seeds[5], 71), 0)
    rand_blocks = draw_rand_blocks(jax.random.fold_in(seeds[5], 71), 0)
    global_ids = jax.random.randint(seeds[4], (GLOB,), 0, NB).astype(jnp.int32)
    return {"queries": queries, "key_value": key_value, "lanczos_vec": lanczos_vec, "rand_blocks": rand_blocks, "global_ids": global_ids}


def reference(queries, key_value, lanczos_vec, rand_blocks, global_ids):
    score_scale = HD ** (-0.5)
    block_ids = jnp.arange(NB, dtype=jnp.int32)
    window_part = block_ids[:, None] + jnp.arange(-1, 2, dtype=jnp.int32)[None, :]
    global_part = jnp.broadcast_to(global_ids[None, :], (NB, GLOB)).astype(jnp.int32)
    key_table = jnp.concatenate([window_part, global_part, rand_blocks.astype(jnp.int32)], axis=1)
    window_ok = (window_part >= 0) & (window_part < NB)
    valid_table = jnp.concatenate([window_ok, jnp.ones((NB, GLOB + RAND), dtype=bool)], axis=1)
    key_table = jnp.clip(key_table, 0, NB - 1).astype(jnp.int32)
    tangent_all = lanczos_vec.astype(jnp.bfloat16)

    def one_block(block):
        block_row = key_table[block]
        valid_row = valid_table[block]
        token_index = (block_row[:, None] * BS + jnp.arange(BS, dtype=jnp.int32)[None, :]).reshape(-1)
        keys = jnp.take(key_value[0], token_index, axis=0).astype(jnp.float32).reshape(-1, HEADS, HD)
        values = jnp.take(key_value[1], token_index, axis=0).astype(jnp.float32).reshape(-1, HEADS, HD)
        start = (block * BS).astype(jnp.int32)
        query = lax.dynamic_slice_in_dim(queries, start, BS, 0).astype(jnp.float32).reshape(BS, HEADS, HD)
        tangent = lax.dynamic_slice_in_dim(tangent_all, start, BS, 0).astype(jnp.float32).reshape(BS, HEADS, HD)
        valid_keys = jnp.repeat(valid_row, BS)[None, None, :]
        scores = jnp.einsum('qhd,khd->hqk', query, keys) * score_scale
        row_top = lax.optimization_barrier(jnp.max(jnp.where(valid_keys, scores, -jnp.inf), axis=-1, keepdims=True))
        weights = jnp.where(valid_keys, jnp.exp(scores - row_top), 0.0)
        attention = weights / lax.optimization_barrier(jnp.sum(weights, axis=-1, keepdims=True))
        dscore = jnp.einsum('qhd,khd->hqk', tangent, keys) * score_scale
        center = lax.optimization_barrier(jnp.sum(attention * dscore, axis=-1, keepdims=True))
        first_grad = lax.optimization_barrier((attention * (dscore - center)).astype(jnp.bfloat16)).astype(jnp.float32)
        tangent_out = jnp.einsum('hqk,khd->qhd', first_grad, values)
        tangent_out = lax.optimization_barrier(tangent_out.astype(jnp.bfloat16)).astype(jnp.float32)
        back_prob = jnp.einsum('qhd,khd->hqk', tangent_out, values)
        center_two = lax.optimization_barrier(jnp.sum(attention * back_prob, axis=-1, keepdims=True))
        second_grad = lax.optimization_barrier((attention * (back_prob - center_two)).astype(jnp.bfloat16)).astype(jnp.float32)
        image = jnp.einsum('hqk,khd->qhd', second_grad, keys) * score_scale
        return image.reshape(BS, HEADS * HD)
    product = lax.map(one_block, block_ids).reshape(SEQ, DM)
    entry_count = float(SEQ * DM)
    alpha_coef = jnp.sum(lanczos_vec * product) / entry_count
    residual = product - alpha_coef * lanczos_vec
    beta_coef = jnp.sqrt(jnp.sum(residual * residual) / entry_count + 1e-06)
    return (residual / beta_coef, jnp.stack([alpha_coef, beta_coef]))
```

```python
import functools

import jax
import jax.numpy as jnp
from jax import lax
from jax.experimental import pallas as pl
from jax.experimental.pallas import tpu as pltpu
from jax.sharding import PartitionSpec as P

HD = 128
BS = 128
SCALE = HD ** (-0.5)
LOG2E = 1.4426950408889634
NEG = float("-inf")
CHUNKS = 4
VMEM_LIMIT = 56 * 1024 * 1024


def attend(q, t, keys, vals, biases):
    k = jnp.concatenate(keys, axis=0)
    v = jnp.concatenate(vals, axis=0)
    nt = (((1,), (1,)), ((), ()))
    nn = (((1,), (0,)), ((), ()))
    both = lax.dot_general(
        jnp.concatenate([q, t.astype(jnp.bfloat16)], axis=0), k, nt,
        preferred_element_type=jnp.float32,
    )
    s = both[:BS]
    ds = both[BS:]
    parts = []
    for i in range(len(keys)):
        part = s[:, i * BS : (i + 1) * BS]
        parts.append(part if biases[i] is None else part + biases[i])
    s = jnp.concatenate(parts, axis=1)
    top = jnp.max(s, axis=1, keepdims=True)
    w = jnp.exp2((s - top) * (SCALE * LOG2E))
    inv = 1.0 / jnp.sum(w, axis=1, keepdims=True)
    p = w * inv
    center = jnp.sum(p * ds, axis=1, keepdims=True)
    g = ((p * SCALE) * (ds - center)).astype(jnp.bfloat16)
    dout = lax.dot_general(g, v, nn, preferred_element_type=jnp.float32).astype(jnp.bfloat16)
    dp = lax.dot_general(dout, v, nt, preferred_element_type=jnp.float32)
    center2 = jnp.sum(p * dp, axis=1, keepdims=True)
    g2 = (p * (dp - center2)).astype(jnp.bfloat16)
    return lax.dot_general(g2, k, nn, preferred_element_type=jnp.float32) * SCALE


def fold(x):
    return jnp.sum(x.reshape(BS // 8, 8, HD), axis=0)


def attend_kernel(nblocks, rand, slots, edge, q_ref, t_ref, kv_ref, lo_ref, hi_ref, gl_ref, in_ref, *rest):
    out_ref, sum_ref = rest[-2:]
    h = pl.program_id(0)

    @pl.when(h == 0)
    def _():
        sum_ref[...] = jnp.zeros_like(sum_ref)

    def block(b):
        rows = pl.ds(b * BS, BS)

        def listed(i):
            got = []
            if b == 0:
                got.append(lo_ref[i])
            else:
                got.append(kv_ref[i, (b - 1) * BS : b * BS, :])
            got.append(kv_ref[i, b * BS : (b + 1) * BS, :])
            if b == nblocks - 1:
                got.append(hi_ref[i])
            else:
                got.append(kv_ref[i, (b + 1) * BS : (b + 2) * BS, :])
            for g in range(gl_ref.shape[1] // BS):
                got.append(gl_ref[i, g * BS : (g + 1) * BS, :])
            for r in range(rand):
                got.append(in_ref[slots[b * rand + r], i])
            return got

        keys, vals = listed(0), listed(1)
        biases = [None] * len(keys)
        if b == 0:
            biases[0] = jnp.where(edge[0] > 0, NEG, 0.0).astype(jnp.float32)
        if b == nblocks - 1:
            biases[2] = jnp.where(edge[1] > 0, NEG, 0.0).astype(jnp.float32)
        t = t_ref[rows, :]
        image = attend(q_ref[rows, :], t, keys, vals, biases)
        out_ref[rows, :] = image
        sum_ref[0] += fold(t * image)
        sum_ref[1] += fold(image * image)
        sum_ref[2] += fold(t * t)

    for b in range(nblocks):
        block(b)


def attend_chunk(c, heads, queries, vec, key_value, lo, hi, glob, incoming, slots, edge, product):
    rows, width = queries.shape
    nblocks = rows // BS
    nslots = incoming.shape[0]
    rand = slots.shape[0] // nblocks
    first = c * heads
    col = lambda h, *_: (0, first + h)
    col3 = lambda h, *_: (0, 0, first + h)
    in_specs = [
        pl.BlockSpec((rows, HD), col),
        pl.BlockSpec((rows, HD), col),
        pl.BlockSpec((2, rows, HD), col3),
        pl.BlockSpec((2, BS, HD), col3),
        pl.BlockSpec((2, BS, HD), col3),
        pl.BlockSpec((2, glob.shape[1], HD), col3),
        pl.BlockSpec((nslots, 2, BS, HD), lambda h, *_: (0, 0, 0, h)),
    ]
    args = [slots, edge, queries, vec, key_value, lo, hi, glob, incoming]
    aliases = {}
    if product is not None:
        in_specs.append(pl.BlockSpec(memory_space=pl.ANY))
        aliases = {len(args): 0}
        args.append(product)
    return pl.pallas_call(
        functools.partial(attend_kernel, nblocks, rand),
        grid_spec=pltpu.PrefetchScalarGridSpec(
            num_scalar_prefetch=2,
            grid=(heads,),
            in_specs=in_specs,
            out_specs=[
                pl.BlockSpec((rows, HD), col),
                pl.BlockSpec((3, 8, HD), lambda h, *_: (0, 0, 0)),
            ],
        ),
        out_shape=[
            jax.ShapeDtypeStruct((rows, width), jnp.float32),
            jax.ShapeDtypeStruct((3, 8, HD), jnp.float32),
        ],
        input_output_aliases=aliases,
        compiler_params=pltpu.CompilerParams(vmem_limit_bytes=VMEM_LIMIT),
        cost_estimate=pl.CostEstimate(
            flops=heads * nblocks * 5 * 2 * BS * HD * 8 * BS * 4, bytes_accessed=heads * 8 * 2**20, transcendentals=0
        ),
    )(*args)


def pick_kernel(chosen, kv_ref, *outs):
    width = outs[0].shape[-1]
    for c, out in enumerate(outs):
        out[0] = kv_ref[:, :, c * width : (c + 1) * width]


def pick_blocks(key_value, chosen):
    count = chosen.shape[0]
    cols = key_value.shape[2]
    width = cols // CHUNKS
    return pl.pallas_call(
        pick_kernel,
        grid_spec=pltpu.PrefetchScalarGridSpec(
            num_scalar_prefetch=1,
            grid=(count,),
            in_specs=[pl.BlockSpec((2, BS, cols), lambda i, chosen: (0, chosen[i], 0))],
            out_specs=[pl.BlockSpec((1, 2, BS, width), lambda i, chosen: (i, 0, 0, 0))] * CHUNKS,
        ),
        out_shape=[jax.ShapeDtypeStruct((count, 2, BS, width), key_value.dtype)] * CHUNKS,
    )(chosen, key_value)


def from_root(block, axis, holder):
    block = jnp.where(lax.axis_index(axis) == holder, block, jnp.zeros_like(block))
    return lax.psum(block, axis)


def request_tables(rand_blocks, nblocks, ctx_count, ctx_index, capacity):
    requests = rand_blocks.reshape(ctx_count, -1)
    sources = requests // nblocks
    inside = requests % nblocks
    mine = (sources == ctx_index).astype(jnp.int32)
    earlier = jnp.cumsum(mine, axis=1) - mine
    slot_ids = jnp.arange(capacity, dtype=jnp.int32)
    matched = (mine[:, :, None] == 1) & (earlier[:, :, None] == slot_ids[None, None, :])
    chosen = jnp.sum(jnp.where(matched, inside[:, :, None], 0), axis=1).reshape(-1)
    own = lax.dynamic_index_in_dim(sources, ctx_index, 0, keepdims=False)
    total = own.shape[0]
    before = jnp.arange(total)[:, None] > jnp.arange(total)[None, :]
    same = own[:, None] == own[None, :]
    rank = jnp.sum((before & same).astype(jnp.int32), axis=1)
    return chosen, own * capacity + rank


def local(queries, key_value, lanczos_vec, rand_blocks, global_ids):
    rows, cols = queries.shape
    nblocks = rows // BS
    n = lax.axis_size("ctx")
    me = lax.axis_index("ctx")
    rand = rand_blocks.shape[1]
    capacity = (nblocks * rand + n - 1) // n
    chosen, slots = request_tables(rand_blocks, nblocks, n, me, capacity)
    outgoing = pick_blocks(key_value, chosen)
    incoming = [lax.all_to_all(part, "ctx", split_axis=0, concat_axis=0, tiled=True) for part in outgoing]
    lo = lax.ppermute(key_value[:, rows - BS :], "ctx", [(i, i + 1) for i in range(n - 1)])
    hi = lax.ppermute(key_value[:, :BS], "ctx", [(i + 1, i) for i in range(n - 1)])
    pieces = []
    for g in range(global_ids.shape[0]):
        piece = lax.dynamic_slice_in_dim(key_value, global_ids[g] % nblocks * BS, BS, 1)
        pieces.append(from_root(piece, "ctx", global_ids[g] // nblocks))
    glob = jnp.concatenate(pieces, axis=1)
    edge = jnp.stack([me == 0, me == n - 1]).astype(jnp.int32)
    product = None
    sums = 0.0
    heads = cols // HD // CHUNKS
    for c in range(CHUNKS):
        product, part = attend_chunk(
            c, heads, queries, lanczos_vec, key_value, lo, hi, glob, incoming[c], slots, edge, product
        )
        sums = sums + part
    count = float(rows * cols * n * lax.axis_size("head"))
    cross, image, vector = jnp.split(lax.psum(jnp.sum(sums, axis=(1, 2)), ("ctx", "head")), 3)
    alpha = cross[0] / count
    square = image[0] - 2.0 * alpha * cross[0] + alpha * alpha * vector[0]
    beta = jnp.sqrt(square / count + 1e-06)
    return (product - alpha * lanczos_vec) / beta, jnp.stack([alpha, beta])


def solution(mesh):
    placed = (P("ctx", "head"), P(None, "ctx", "head"), P("ctx", "head"), P(), P())
    return jax.shard_map(
        local, mesh=mesh, in_specs=placed, out_specs=(P("ctx", "head"), P()), check_vma=False
    )
```

```python
import functools

import jax
import jax.numpy as jnp
from jax import lax
from jax.experimental import pallas as pl
from jax.experimental.pallas import tpu as pltpu
from jax.sharding import PartitionSpec as P

HD = 128
BS = 128
SCALE = HD ** (-0.5)
LOG2E = 1.4426950408889634
NEG = float("-inf")
CHUNKS = 4
VMEM_LIMIT = 56 * 1024 * 1024
NZ = 4
NY = 2
MESH = pl.DeviceIdType.MESH


def attend(q, t, keys, vals, biases):
    k = jnp.concatenate(keys, axis=0)
    v = jnp.concatenate(vals, axis=0)
    nt = (((1,), (1,)), ((), ()))
    nn = (((1,), (0,)), ((), ()))
    both = lax.dot_general(
        jnp.concatenate([q, t.astype(jnp.bfloat16)], axis=0), k, nt,
        preferred_element_type=jnp.float32,
    )
    s = both[:BS]
    ds = both[BS:]
    parts = []
    for i in range(len(keys)):
        part = s[:, i * BS : (i + 1) * BS]
        parts.append(part if biases[i] is None else part + biases[i])
    s = jnp.concatenate(parts, axis=1)
    top = jnp.max(s, axis=1, keepdims=True)
    w = jnp.exp2((s - top) * (SCALE * LOG2E))
    inv = 1.0 / jnp.sum(w, axis=1, keepdims=True)
    p = w * inv
    center = jnp.sum(p * ds, axis=1, keepdims=True)
    g = ((p * SCALE) * (ds - center)).astype(jnp.bfloat16)
    dout = lax.dot_general(g, v, nn, preferred_element_type=jnp.float32).astype(jnp.bfloat16)
    dp = lax.dot_general(dout, v, nt, preferred_element_type=jnp.float32)
    center2 = jnp.sum(p * dp, axis=1, keepdims=True)
    g2 = (p * (dp - center2)).astype(jnp.bfloat16)
    return lax.dot_general(g2, k, nn, preferred_element_type=jnp.float32) * SCALE


def fold(x):
    return jnp.sum(x.reshape(BS // 8, 8, HD), axis=0)


def attend_kernel(nblocks, rand, slots, edge, q_ref, t_ref, kv_ref, lo_ref, hi_ref, gl_ref, in_ref, *rest):
    out_ref, sum_ref = rest[-2:]
    h = pl.program_id(0)

    @pl.when(h == 0)
    def _():
        sum_ref[...] = jnp.zeros_like(sum_ref)

    def block(b):
        rows = pl.ds(b * BS, BS)

        def listed(i):
            got = []
            if b == 0:
                got.append(lo_ref[i])
            else:
                got.append(kv_ref[i, (b - 1) * BS : b * BS, :])
            got.append(kv_ref[i, b * BS : (b + 1) * BS, :])
            if b == nblocks - 1:
                got.append(hi_ref[i])
            else:
                got.append(kv_ref[i, (b + 1) * BS : (b + 2) * BS, :])
            for g in range(gl_ref.shape[1] // BS):
                got.append(gl_ref[i, g * BS : (g + 1) * BS, :])
            for r in range(rand):
                got.append(in_ref[slots[b * rand + r], i])
            return got

        keys, vals = listed(0), listed(1)
        biases = [None] * len(keys)
        if b == 0:
            biases[0] = jnp.where(edge[0] > 0, NEG, 0.0).astype(jnp.float32)
        if b == nblocks - 1:
            biases[2] = jnp.where(edge[1] > 0, NEG, 0.0).astype(jnp.float32)
        t = t_ref[rows, :]
        image = attend(q_ref[rows, :], t, keys, vals, biases)
        out_ref[rows, :] = image
        sum_ref[0] += fold(t * image)
        sum_ref[1] += fold(image * image)
        sum_ref[2] += fold(t * t)

    for b in range(nblocks):
        block(b)


def attend_chunk(c, heads, queries, vec, key_value, lo, hi, glob, incoming, slots, edge, product):
    rows, width = queries.shape
    nblocks = rows // BS
    nslots = incoming.shape[0]
    rand = slots.shape[0] // nblocks
    first = c * heads
    col = lambda h, *_: (0, first + h)
    col3 = lambda h, *_: (0, 0, first + h)
    in_specs = [
        pl.BlockSpec((rows, HD), col),
        pl.BlockSpec((rows, HD), col),
        pl.BlockSpec((2, rows, HD), col3),
        pl.BlockSpec((2, BS, HD), col3),
        pl.BlockSpec((2, BS, HD), col3),
        pl.BlockSpec((2, glob.shape[1], HD), col3),
        pl.BlockSpec((nslots, 2, BS, HD), lambda h, *_: (0, 0, 0, h)),
    ]
    args = [slots, edge, queries, vec, key_value, lo, hi, glob, incoming]
    aliases = {}
    if product is not None:
        in_specs.append(pl.BlockSpec(memory_space=pl.ANY))
        aliases = {len(args): 0}
        args.append(product)
    return pl.pallas_call(
        functools.partial(attend_kernel, nblocks, rand),
        grid_spec=pltpu.PrefetchScalarGridSpec(
            num_scalar_prefetch=2,
            grid=(heads,),
            in_specs=in_specs,
            out_specs=[
                pl.BlockSpec((rows, HD), col),
                pl.BlockSpec((3, 8, HD), lambda h, *_: (0, 0, 0)),
            ],
        ),
        out_shape=[
            jax.ShapeDtypeStruct((rows, width), jnp.float32),
            jax.ShapeDtypeStruct((3, 8, HD), jnp.float32),
        ],
        input_output_aliases=aliases,
        compiler_params=pltpu.CompilerParams(vmem_limit_bytes=VMEM_LIMIT),
        cost_estimate=pl.CostEstimate(
            flops=heads * nblocks * 5 * 2 * BS * HD * 8 * BS * 4, bytes_accessed=heads * 8 * 2**20, transcendentals=0
        ),
    )(*args)


def pick_kernel(chosen, kv_ref, *outs):
    width = outs[0].shape[-1]
    for c, out in enumerate(outs):
        out[0] = kv_ref[:, :, c * width : (c + 1) * width]


def pick_blocks(key_value, chosen):
    count = chosen.shape[0]
    cols = key_value.shape[2]
    width = cols // CHUNKS
    return pl.pallas_call(
        pick_kernel,
        grid_spec=pltpu.PrefetchScalarGridSpec(
            num_scalar_prefetch=1,
            grid=(count,),
            in_specs=[pl.BlockSpec((2, BS, cols), lambda i, chosen: (0, chosen[i], 0))],
            out_specs=[pl.BlockSpec((1, 2, BS, width), lambda i, chosen: (i, 0, 0, 0))] * CHUNKS,
        ),
        out_shape=[jax.ShapeDtypeStruct((count, 2, BS, width), key_value.dtype)] * CHUNKS,
    )(chosen, key_value)


def from_root(block, axis, holder):
    block = jnp.where(lax.axis_index(axis) == holder, block, jnp.zeros_like(block))
    return lax.psum(block, axis)


def request_tables(rand_blocks, nblocks, ctx_count, ctx_index, capacity):
    requests = rand_blocks.reshape(ctx_count, -1)
    sources = requests // nblocks
    inside = requests % nblocks
    mine = (sources == ctx_index).astype(jnp.int32)
    earlier = jnp.cumsum(mine, axis=1) - mine
    slot_ids = jnp.arange(capacity, dtype=jnp.int32)
    matched = (mine[:, :, None] == 1) & (earlier[:, :, None] == slot_ids[None, None, :])
    chosen = jnp.sum(jnp.where(matched, inside[:, :, None], 0), axis=1).reshape(-1)
    own = lax.dynamic_index_in_dim(sources, ctx_index, 0, keepdims=False)
    total = own.shape[0]
    before = jnp.arange(total)[:, None] > jnp.arange(total)[None, :]
    same = own[:, None] == own[None, :]
    rank = jnp.sum((before & same).astype(jnp.int32), axis=1)
    return chosen, own * capacity + rank


def local(queries, key_value, lanczos_vec, rand_blocks, global_ids):
    rows, cols = queries.shape
    nblocks = rows // BS
    n = lax.axis_size("ctx")
    me = lax.axis_index("ctx")
    rand = rand_blocks.shape[1]
    capacity = (nblocks * rand + n - 1) // n
    chosen, slots = request_tables(rand_blocks, nblocks, n, me, capacity)
    outgoing = pick_blocks(key_value, chosen)
    incoming = [lax.all_to_all(part, "ctx", split_axis=0, concat_axis=0, tiled=True) for part in outgoing]
    lo = lax.ppermute(key_value[:, rows - BS :], "ctx", [(i, i + 1) for i in range(n - 1)])
    hi = lax.ppermute(key_value[:, :BS], "ctx", [(i + 1, i) for i in range(n - 1)])
    pieces = []
    for g in range(global_ids.shape[0]):
        piece = lax.dynamic_slice_in_dim(key_value, global_ids[g] % nblocks * BS, BS, 1)
        pieces.append(from_root(piece, "ctx", global_ids[g] // nblocks))
    glob = jnp.concatenate(pieces, axis=1)
    edge = jnp.stack([me == 0, me == n - 1]).astype(jnp.int32)
    product = None
    sums = 0.0
    heads = cols // HD // CHUNKS
    for c in range(CHUNKS):
        product, part = attend_chunk(
            c, heads, queries, lanczos_vec, key_value, lo, hi, glob, incoming[c], slots, edge, product
        )
        sums = sums + part
    totals = lax.psum(jnp.sum(sums, axis=(1, 2)), ("ctx", "head"))
    return finish(product, lanczos_vec, totals, float(rows * cols * n * lax.axis_size("head")))


def finish(product, vec, totals, count):
    cross, image, vector = totals[0], totals[1], totals[2]
    alpha = cross / count
    square = image - 2.0 * alpha * cross + alpha * alpha * vector
    beta = jnp.sqrt(square / count + 1e-06)
    return (product - alpha * vec) / beta, jnp.stack([alpha, beta])


def line_kernel(dims, tab, q_ref, t_ref, kv_ref, out_ref, sum_ref, *scratch):
    nb, heads, rand, nglob, cap, keep, nctx, nhead = dims
    rowbufs = scratch[:heads]
    ybufs = scratch[heads : 2 * heads]
    (pool, ysend, left_order, glbuf, halo, red1, red2, right_s, right_r, left_s, left_r,
     y_s, y_r, gl_s, gl_r, halo_s, halo_r, red_s, red_r) = scratch[2 * heads :]
    ny_slots = NZ * cap
    o_right, o_left = 0, nb
    o_y = 2 * nb
    o_g = o_y + ny_slots
    o_gl = o_g + nglob
    o_r = o_gl + nglob
    me = lax.axis_index("ctx")
    hd = lax.axis_index("head")
    z = me // NY
    y = me % NY
    peer = z * NY + (NY - 1 - y)
    last = NZ - 1

    barrier = pltpu.get_barrier_semaphore()
    for o in range(1, nctx):
        pl.semaphore_signal(barrier, inc=1, device_id={"ctx": lax.rem(me + o, nctx)}, device_id_type=MESH)
    for o in range(1, nhead):
        pl.semaphore_signal(barrier, inc=1, device_id={"head": lax.rem(hd + o, nhead)}, device_id_type=MESH)

    def cols(c):
        return slice(c * HD, (c + 1) * HD)

    def hop(c, right, s, count):
        pos_z = z - s if right else z + s
        place = pl.ds(pos_z * nb, count)
        target = me + NY if right else me - NY
        if s == 0 and not right:
            source = left_order.at[c % 2, pl.ds(0, count)]
        else:
            source = rowbufs[c].at[place]
        ss, rr = (right_s, right_r) if right else (left_s, left_r)
        return pltpu.make_async_remote_copy(
            src_ref=source, dst_ref=rowbufs[c].at[place], send_sem=ss.at[c, s], recv_sem=rr.at[c, s],
            device_id={"ctx": target}, device_id_type=MESH,
        )

    def each_hop(c, right, s, act):
        pos = z if right else last - z

        @pl.when((pos >= s) & (pos < last - 1))
        def _():
            act(hop(c, right, s, nb))

        @pl.when(pos == last - 1)
        def _():
            if s <= last - 1:
                act(hop(c, right, s, keep))

    def arrive(c, right, s):
        pos = z if right else last - z
        src_z = z - s - 1 if right else z + s + 1
        ss, rr = (right_s, right_r) if right else (left_s, left_r)

        def wait(count):
            place = rowbufs[c].at[pl.ds(src_z * nb, count)]
            pltpu.make_async_remote_copy(
                src_ref=place, dst_ref=place, send_sem=ss.at[c, s], recv_sem=rr.at[c, s],
                device_id={"ctx": peer}, device_id_type=MESH,
            ).wait_recv()

        @pl.when((pos >= s + 1) & (pos < last))
        def _():
            wait(nb)

        @pl.when(pos == last)
        def _():
            wait(keep)

    def halo_copy(c, up):
        block = nb - 1 if up else 0
        i = 0 if up else 1
        return pltpu.make_async_remote_copy(
            src_ref=kv_ref.at[:, block, :, cols(c)], dst_ref=halo.at[c, i],
            send_sem=halo_s.at[c, i], recv_sem=halo_r.at[c, i],
            device_id={"ctx": me + 1 if up else me - 1}, device_id_type=MESH,
        )

    def y_copy(c):
        return pltpu.make_async_remote_copy(
            src_ref=ysend.at[c % 2], dst_ref=ybufs[c], send_sem=y_s.at[c], recv_sem=y_r.at[c],
            device_id={"ctx": peer}, device_id_type=MESH,
        )

    def gl_copy(c, right):
        return pltpu.make_async_remote_copy(
            src_ref=ysend.at[c % 2, pl.ds(ny_slots, nglob)], dst_ref=glbuf.at[c],
            send_sem=gl_s.at[c], recv_sem=gl_r.at[c],
            device_id={"ctx": me + NY if right else me - NY}, device_id_type=MESH,
        )

    def each_gl(c, act):
        @pl.when(z == last - 1)
        def _():
            act(gl_copy(c, True))

        @pl.when(z == 1)
        def _():
            act(gl_copy(c, False))

    def own_left_sent(c):
        each_hop(c, False, 0, lambda copy: copy.wait_send())

    def begin(c):
        if c >= 2:
            own_left_sent(c - 2)
        for i in range(nb):
            rowbufs[c][z * nb + i] = kv_ref[:, tab[o_right + i], :, cols(c)]
            left_order[c % 2, i] = kv_ref[:, tab[o_left + i], :, cols(c)]
        each_hop(c, True, 0, lambda copy: copy.start())
        each_hop(c, False, 0, lambda copy: copy.start())

        @pl.when(me < nctx - 1)
        def _():
            halo_copy(c, True).start()

        @pl.when(me > 0)
        def _():
            halo_copy(c, False).start()

        @pl.when(me == 0)
        def _():
            halo[c, 0] = jnp.zeros(halo.shape[2:], halo.dtype)

        @pl.when(me == nctx - 1)
        def _():
            halo[c, 1] = jnp.zeros(halo.shape[2:], halo.dtype)

    def relay(c, s):
        arrive(c, True, s - 1)
        arrive(c, False, s - 1)
        if s < last:
            each_hop(c, True, s, lambda copy: copy.start())
            each_hop(c, False, s, lambda copy: copy.start())

    def across(c):
        if c >= 2:
            y_copy(c - 2).wait_send()
            each_gl(c - 2, lambda copy: copy.wait_send())
        pool[: NZ * nb] = rowbufs[c][...]

        @pl.when((z == 0) | (z == last))
        def _():
            gl_copy(c, True).wait_recv()
            pool[NZ * nb + ny_slots + nglob :] = glbuf[c]

        for g in range(nglob):
            ysend[c % 2, ny_slots + g] = pool[tab[o_g + g]]
        each_gl(c, lambda copy: copy.start())
        for i in range(ny_slots):
            ysend[c % 2, i] = pool[tab[o_y + i]]
        y_copy(c).start()

    def compute(c):
        y_copy(c).wait_recv()
        pool[NZ * nb : NZ * nb + ny_slots + nglob] = ybufs[c][...]

        @pl.when(me > 0)
        def _():
            halo_copy(c, True).wait_recv()

        @pl.when(me < nctx - 1)
        def _():
            halo_copy(c, False).wait_recv()

        def body(b, carry):
            def own(i):
                return kv_ref[:, i, :, cols(c)]

            got = [
                lax.select(b == 0, halo[c, 0], own(jnp.maximum(b - 1, 0))),
                own(b),
                lax.select(b == nb - 1, halo[c, 1], own(jnp.minimum(b + 1, nb - 1))),
            ]
            for g in range(nglob):
                got.append(pool[tab[o_gl + g]])
            for r in range(rand):
                got.append(pool[tab[o_r + b * rand + r]])
            biases = [None] * len(got)
            biases[0] = jnp.where((b == 0) & (me == 0), NEG, 0.0).astype(jnp.float32)
            biases[2] = jnp.where((b == nb - 1) & (me == nctx - 1), NEG, 0.0).astype(jnp.float32)
            rows = pl.ds(pl.multiple_of(b * BS, BS), BS)
            t = t_ref[rows, cols(c)]
            image = attend(q_ref[rows, cols(c)], t, [x[0] for x in got], [x[1] for x in got], biases)
            out_ref[rows, cols(c)] = image
            sum_ref[0] += fold(t * image)
            sum_ref[1] += fold(image * image)
            sum_ref[2] += fold(t * t)
            return carry

        lax.fori_loop(0, nb, body, 0)

    pl.semaphore_wait(barrier, nctx - 1 + nhead - 1)
    sum_ref[...] = jnp.zeros_like(sum_ref)
    begin(0)
    for c in range(heads):
        if c + 1 < heads:
            begin(c + 1)
        relay(c, 1)
        if c >= 1:
            compute(c - 1)
        relay(c, 2)
        relay(c, 3)
        across(c)
    compute(heads - 1)

    def share(buf, axis, mine, count, base):
        buf[mine] = sum_ref[...]
        copies = []
        for o in range(1, count):
            copy = pltpu.make_async_remote_copy(
                src_ref=buf.at[mine], dst_ref=buf.at[mine],
                send_sem=red_s.at[base + o - 1], recv_sem=red_r.at[base + o - 1],
                device_id={axis: lax.rem(mine + o, count)}, device_id_type=MESH,
            )
            copy.start()
            copies.append(copy)
        for o in range(1, count):
            place = buf.at[lax.rem(mine + count - o, count)]
            pltpu.make_async_remote_copy(
                src_ref=place, dst_ref=place,
                send_sem=red_s.at[base + o - 1], recv_sem=red_r.at[base + o - 1],
                device_id={axis: lax.rem(mine + o, count)}, device_id_type=MESH,
            ).wait_recv()
        total = buf[0]
        for i in range(1, count):
            total = total + buf[i]
        sum_ref[...] = total
        for copy in copies:
            copy.wait_send()

    share(red1, "head", hd, nhead, 0)
    share(red2, "ctx", me, nctx, nhead - 1)

    for c in range(heads):
        for s in range(last):
            each_hop(c, True, s, lambda copy: copy.wait_send())
            if s > 0 or c >= heads - 2:
                each_hop(c, False, s, lambda copy: copy.wait_send())

        @pl.when(me < nctx - 1)
        def _():
            halo_copy(c, True).wait_send()

        @pl.when(me > 0)
        def _():
            halo_copy(c, False).wait_send()

        if c >= heads - 2:
            y_copy(c).wait_send()
            each_gl(c, lambda copy: copy.wait_send())


def line_tables(rand_blocks, global_ids, nb, me, cap, keep):
    n = NZ * NY
    z, y = me // NY, me % NY
    requests = rand_blocks.reshape(n, -1)
    wanted = (requests[:, None, :] == jnp.arange(n * nb, dtype=jnp.int32)[None, :, None]).any(axis=2)
    layer = wanted.reshape(NZ, NY, n * nb).any(axis=1)

    def order(need):
        need = need.reshape(n, nb).astype(jnp.int32)
        first = jnp.cumsum(need, axis=1)
        rest = jnp.cumsum(1 - need, axis=1)
        rank = jnp.where(need == 1, first - 1, first[:, -1:] + rest - 1)
        return rank

    rank_r = order(layer[NZ - 1])
    rank_l = order(layer[0])
    ids = jnp.arange(nb, dtype=jnp.int32)

    def inverse(rank):
        mine = lax.dynamic_index_in_dim(rank, me, 0, keepdims=False)
        return jnp.sum(jnp.where(mine[None, :] == ids[:, None], ids[None, :], 0), axis=1)

    src_z = jnp.arange(n, dtype=jnp.int32) // NY
    rank = jnp.where((src_z <= z)[:, None], rank_r, rank_l)
    place = (src_z[:, None] * nb + rank).reshape(-1)

    def lookup(blocks):
        hit = blocks[:, None] == jnp.arange(n * nb, dtype=jnp.int32)[None, :]
        return jnp.sum(jnp.where(hit, place[None, :], 0), axis=1)

    def ranks(req):
        source = req // nb
        total = req.shape[0]
        before = jnp.arange(total)[:, None] > jnp.arange(total)[None, :]
        return jnp.sum((before & (source[:, None] == source[None, :])).astype(jnp.int32), axis=1)

    own = lax.dynamic_index_in_dim(requests, me, 0, keepdims=False)
    other = lax.dynamic_index_in_dim(requests, z * NY + (NY - 1 - y), 0, keepdims=False)
    other_src = other // nb
    other_slot = jnp.where(other_src % NY == y, (other_src // NY) * cap + ranks(other), -1)
    slot = jnp.arange(NZ * cap, dtype=jnp.int32)
    y_src = jnp.sum(jnp.where(other_slot[None, :] == slot[:, None], lookup(other)[None, :], 0), axis=1)
    g_owner = global_ids // nb
    g_ids = jnp.arange(global_ids.shape[0], dtype=jnp.int32)
    far = ((z == 0) | (z == NZ - 1)) & (g_owner // NY != z)
    y_base = NZ * nb
    g_base = y_base + NZ * cap
    g_src = jnp.where(far, g_base + g_ids.shape[0] + g_ids, lookup(global_ids))
    g_all = jnp.where(g_owner % NY == y, g_src, g_base + g_ids)
    own_src = own // nb
    r_all = jnp.where(own_src % NY == y, lookup(own), y_base + (own_src // NY) * cap + ranks(own))
    parts = [inverse(rank_r), inverse(rank_l), y_src, g_src, g_all, r_all]
    return jnp.concatenate([p.astype(jnp.int32) for p in parts])


def line_local(queries, key_value, lanczos_vec, rand_blocks, global_ids):
    rows, cols = queries.shape
    nb = rows // BS
    heads = cols // HD
    n = lax.axis_size("ctx")
    nhead = lax.axis_size("head")
    me = lax.axis_index("ctx")
    rand = rand_blocks.shape[1]
    nglob = global_ids.shape[0]
    cap = (nb * rand + n - 1) // n
    keep = min(nb, NY * cap)
    tab = line_tables(rand_blocks, global_ids, nb, me, cap, keep)
    slots = NZ * cap + nglob
    dims = (nb, heads, rand, nglob, cap, keep, n, nhead)
    unit = (2, BS, HD)
    vmem = pl.BlockSpec(memory_space=pltpu.VMEM)
    sem = pltpu.SemaphoreType.DMA
    product, sums = pl.pallas_call(
        functools.partial(line_kernel, dims),
        in_specs=[pl.BlockSpec(memory_space=pltpu.SMEM), vmem, vmem, vmem],
        out_specs=[vmem, vmem],
        out_shape=[
            jax.ShapeDtypeStruct((rows, cols), jnp.float32),
            jax.ShapeDtypeStruct((3, 8, HD), jnp.float32),
        ],
        scratch_shapes=[pltpu.VMEM((NZ * nb,) + unit, jnp.bfloat16)] * heads
        + [pltpu.VMEM((slots,) + unit, jnp.bfloat16)] * heads
        + [
            pltpu.VMEM((NZ * nb + slots + nglob,) + unit, jnp.bfloat16),
            pltpu.VMEM((2, slots) + unit, jnp.bfloat16),
            pltpu.VMEM((2, nb) + unit, jnp.bfloat16),
            pltpu.VMEM((heads, nglob) + unit, jnp.bfloat16),
            pltpu.VMEM((heads, 2) + unit, jnp.bfloat16),
            pltpu.VMEM((nhead, 3, 8, HD), jnp.float32),
            pltpu.VMEM((n, 3, 8, HD), jnp.float32),
            sem((heads, NZ)), sem((heads, NZ)), sem((heads, NZ)), sem((heads, NZ)),
            sem((heads,)), sem((heads,)), sem((heads,)), sem((heads,)),
            sem((heads, 2)), sem((heads, 2)),
            sem((n + nhead,)), sem((n + nhead,)),
        ],
        compiler_params=pltpu.CompilerParams(
            collective_id=0, has_side_effects=True, vmem_limit_bytes=VMEM_LIMIT
        ),
    )(tab, queries, lanczos_vec, key_value.reshape(2, nb, BS, cols))
    return finish(product, lanczos_vec, jnp.sum(sums, axis=(1, 2)), float(rows * cols * n * nhead))


def solution(mesh):
    placed = (P("ctx", "head"), P(None, "ctx", "head"), P("ctx", "head"), P(), P())
    body = line_local if mesh.shape["ctx"] == NZ * NY else local
    return jax.shard_map(
        body, mesh=mesh, in_specs=placed, out_specs=(P("ctx", "head"), P()), check_vma=False
    )
```

```python
import functools

import jax
import jax.numpy as jnp
from jax import lax
from jax.experimental import pallas as pl
from jax.experimental.pallas import tpu as pltpu
from jax.sharding import PartitionSpec as P

HD = 128
BS = 128
SCALE = HD ** (-0.5)
LOG2E = 1.4426950408889634
NEG = float("-inf")
CHUNKS = 4
VMEM_LIMIT = 56 * 1024 * 1024
NZ = 4
NY = 2
MESH = pl.DeviceIdType.MESH


def attend(q, t, keys, vals, biases):
    k = jnp.concatenate(keys, axis=0)
    v = jnp.concatenate(vals, axis=0)
    nt = (((1,), (1,)), ((), ()))
    nn = (((1,), (0,)), ((), ()))
    both = lax.dot_general(
        jnp.concatenate([q, t.astype(jnp.bfloat16)], axis=0), k, nt,
        preferred_element_type=jnp.float32,
    )
    s = both[:BS]
    ds = both[BS:]
    parts = []
    for i in range(len(keys)):
        part = s[:, i * BS : (i + 1) * BS]
        parts.append(part if biases[i] is None else part + biases[i])
    s = jnp.concatenate(parts, axis=1)
    top = jnp.max(s, axis=1, keepdims=True)
    w = jnp.exp2((s - top) * (SCALE * LOG2E))
    inv = 1.0 / jnp.sum(w, axis=1, keepdims=True)
    p = w * inv
    center = jnp.sum(p * ds, axis=1, keepdims=True)
    g = ((p * SCALE) * (ds - center)).astype(jnp.bfloat16)
    dout = lax.dot_general(g, v, nn, preferred_element_type=jnp.float32).astype(jnp.bfloat16)
    dp = lax.dot_general(dout, v, nt, preferred_element_type=jnp.float32)
    center2 = jnp.sum(p * dp, axis=1, keepdims=True)
    g2 = (p * (dp - center2)).astype(jnp.bfloat16)
    return lax.dot_general(g2, k, nn, preferred_element_type=jnp.float32) * SCALE


def fold(x):
    return jnp.sum(x.reshape(BS // 8, 8, HD), axis=0)


def attend_kernel(nblocks, rand, slots, edge, q_ref, t_ref, kv_ref, lo_ref, hi_ref, gl_ref, in_ref, *rest):
    out_ref, sum_ref = rest[-2:]
    h = pl.program_id(0)

    @pl.when(h == 0)
    def _():
        sum_ref[...] = jnp.zeros_like(sum_ref)

    def block(b):
        rows = pl.ds(b * BS, BS)

        def listed(i):
            got = []
            if b == 0:
                got.append(lo_ref[i])
            else:
                got.append(kv_ref[i, (b - 1) * BS : b * BS, :])
            got.append(kv_ref[i, b * BS : (b + 1) * BS, :])
            if b == nblocks - 1:
                got.append(hi_ref[i])
            else:
                got.append(kv_ref[i, (b + 1) * BS : (b + 2) * BS, :])
            for g in range(gl_ref.shape[1] // BS):
                got.append(gl_ref[i, g * BS : (g + 1) * BS, :])
            for r in range(rand):
                got.append(in_ref[slots[b * rand + r], i])
            return got

        keys, vals = listed(0), listed(1)
        biases = [None] * len(keys)
        if b == 0:
            biases[0] = jnp.where(edge[0] > 0, NEG, 0.0).astype(jnp.float32)
        if b == nblocks - 1:
            biases[2] = jnp.where(edge[1] > 0, NEG, 0.0).astype(jnp.float32)
        t = t_ref[rows, :]
        image = attend(q_ref[rows, :], t, keys, vals, biases)
        out_ref[rows, :] = image
        sum_ref[0] += fold(t * image)
        sum_ref[1] += fold(image * image)
        sum_ref[2] += fold(t * t)

    for b in range(nblocks):
        block(b)


def attend_chunk(c, heads, queries, vec, key_value, lo, hi, glob, incoming, slots, edge, product):
    rows, width = queries.shape
    nblocks = rows // BS
    nslots = incoming.shape[0]
    rand = slots.shape[0] // nblocks
    first = c * heads
    col = lambda h, *_: (0, first + h)
    col3 = lambda h, *_: (0, 0, first + h)
    in_specs = [
        pl.BlockSpec((rows, HD), col),
        pl.BlockSpec((rows, HD), col),
        pl.BlockSpec((2, rows, HD), col3),
        pl.BlockSpec((2, BS, HD), col3),
        pl.BlockSpec((2, BS, HD), col3),
        pl.BlockSpec((2, glob.shape[1], HD), col3),
        pl.BlockSpec((nslots, 2, BS, HD), lambda h, *_: (0, 0, 0, h)),
    ]
    args = [slots, edge, queries, vec, key_value, lo, hi, glob, incoming]
    aliases = {}
    if product is not None:
        in_specs.append(pl.BlockSpec(memory_space=pl.ANY))
        aliases = {len(args): 0}
        args.append(product)
    return pl.pallas_call(
        functools.partial(attend_kernel, nblocks, rand),
        grid_spec=pltpu.PrefetchScalarGridSpec(
            num_scalar_prefetch=2,
            grid=(heads,),
            in_specs=in_specs,
            out_specs=[
                pl.BlockSpec((rows, HD), col),
                pl.BlockSpec((3, 8, HD), lambda h, *_: (0, 0, 0)),
            ],
        ),
        out_shape=[
            jax.ShapeDtypeStruct((rows, width), jnp.float32),
            jax.ShapeDtypeStruct((3, 8, HD), jnp.float32),
        ],
        input_output_aliases=aliases,
        compiler_params=pltpu.CompilerParams(vmem_limit_bytes=VMEM_LIMIT),
        cost_estimate=pl.CostEstimate(
            flops=heads * nblocks * 5 * 2 * BS * HD * 8 * BS * 4, bytes_accessed=heads * 8 * 2**20, transcendentals=0
        ),
    )(*args)


def pick_kernel(chosen, kv_ref, *outs):
    width = outs[0].shape[-1]
    for c, out in enumerate(outs):
        out[0] = kv_ref[:, :, c * width : (c + 1) * width]


def pick_blocks(key_value, chosen):
    count = chosen.shape[0]
    cols = key_value.shape[2]
    width = cols // CHUNKS
    return pl.pallas_call(
        pick_kernel,
        grid_spec=pltpu.PrefetchScalarGridSpec(
            num_scalar_prefetch=1,
            grid=(count,),
            in_specs=[pl.BlockSpec((2, BS, cols), lambda i, chosen: (0, chosen[i], 0))],
            out_specs=[pl.BlockSpec((1, 2, BS, width), lambda i, chosen: (i, 0, 0, 0))] * CHUNKS,
        ),
        out_shape=[jax.ShapeDtypeStruct((count, 2, BS, width), key_value.dtype)] * CHUNKS,
    )(chosen, key_value)


def from_root(block, axis, holder):
    block = jnp.where(lax.axis_index(axis) == holder, block, jnp.zeros_like(block))
    return lax.psum(block, axis)


def request_tables(rand_blocks, nblocks, ctx_count, ctx_index, capacity):
    requests = rand_blocks.reshape(ctx_count, -1)
    sources = requests // nblocks
    inside = requests % nblocks
    mine = (sources == ctx_index).astype(jnp.int32)
    earlier = jnp.cumsum(mine, axis=1) - mine
    slot_ids = jnp.arange(capacity, dtype=jnp.int32)
    matched = (mine[:, :, None] == 1) & (earlier[:, :, None] == slot_ids[None, None, :])
    chosen = jnp.sum(jnp.where(matched, inside[:, :, None], 0), axis=1).reshape(-1)
    own = lax.dynamic_index_in_dim(sources, ctx_index, 0, keepdims=False)
    total = own.shape[0]
    before = jnp.arange(total)[:, None] > jnp.arange(total)[None, :]
    same = own[:, None] == own[None, :]
    rank = jnp.sum((before & same).astype(jnp.int32), axis=1)
    return chosen, own * capacity + rank


def local(queries, key_value, lanczos_vec, rand_blocks, global_ids):
    rows, cols = queries.shape
    nblocks = rows // BS
    n = lax.axis_size("ctx")
    me = lax.axis_index("ctx")
    rand = rand_blocks.shape[1]
    capacity = (nblocks * rand + n - 1) // n
    chosen, slots = request_tables(rand_blocks, nblocks, n, me, capacity)
    outgoing = pick_blocks(key_value, chosen)
    incoming = [lax.all_to_all(part, "ctx", split_axis=0, concat_axis=0, tiled=True) for part in outgoing]
    lo = lax.ppermute(key_value[:, rows - BS :], "ctx", [(i, i + 1) for i in range(n - 1)])
    hi = lax.ppermute(key_value[:, :BS], "ctx", [(i + 1, i) for i in range(n - 1)])
    pieces = []
    for g in range(global_ids.shape[0]):
        piece = lax.dynamic_slice_in_dim(key_value, global_ids[g] % nblocks * BS, BS, 1)
        pieces.append(from_root(piece, "ctx", global_ids[g] // nblocks))
    glob = jnp.concatenate(pieces, axis=1)
    edge = jnp.stack([me == 0, me == n - 1]).astype(jnp.int32)
    product = None
    sums = 0.0
    heads = cols // HD // CHUNKS
    for c in range(CHUNKS):
        product, part = attend_chunk(
            c, heads, queries, lanczos_vec, key_value, lo, hi, glob, incoming[c], slots, edge, product
        )
        sums = sums + part
    totals = lax.psum(jnp.sum(sums, axis=(1, 2)), ("ctx", "head"))
    return finish(product, lanczos_vec, totals, float(rows * cols * n * lax.axis_size("head")))


def finish(product, vec, totals, count):
    cross, image, vector = totals[0], totals[1], totals[2]
    alpha = cross / count
    square = image - 2.0 * alpha * cross + alpha * alpha * vector
    beta = jnp.sqrt(square / count + 1e-06)
    return (product - alpha * vec) / beta, jnp.stack([alpha, beta])


def line_kernel(dims, tab, q_ref, t_ref, kv_ref, out_ref, coef_ref, *scratch):
    nb, heads, rand, nglob, cap, keep, nctx, nhead = dims
    rowbufs = scratch[:heads]
    ybufs = scratch[heads : 2 * heads]
    (pool_a, pool_b, sum_ref, ysend, left_order, glbuf, halo, red1, red2, right_s, right_r, left_s, left_r,
     y_s, y_r, gl_s, gl_r, halo_s, halo_r, red_s, red_r) = scratch[2 * heads :]
    pools = (pool_a, pool_b)
    ny_slots = NZ * cap
    o_right, o_left = 0, nb
    o_y = 2 * nb
    o_g = o_y + ny_slots
    o_gl = o_g + nglob
    o_r = o_gl + nglob
    me = lax.axis_index("ctx")
    hd = lax.axis_index("head")
    z = me // NY
    y = me % NY
    peer = z * NY + (NY - 1 - y)
    last = NZ - 1

    barrier = pltpu.get_barrier_semaphore()
    for o in range(1, nctx):
        pl.semaphore_signal(barrier, inc=1, device_id={"ctx": lax.rem(me + o, nctx)}, device_id_type=MESH)
    for o in range(1, nhead):
        pl.semaphore_signal(barrier, inc=1, device_id={"head": lax.rem(hd + o, nhead)}, device_id_type=MESH)

    def cols(c):
        return slice(c * HD, (c + 1) * HD)

    def hop(c, right, s, count):
        pos_z = z - s if right else z + s
        place = pl.ds(pos_z * nb, count)
        target = me + NY if right else me - NY
        if s == 0 and not right:
            source = left_order.at[c % 3, pl.ds(0, count)]
        else:
            source = rowbufs[c].at[place]
        ss, rr = (right_s, right_r) if right else (left_s, left_r)
        return pltpu.make_async_remote_copy(
            src_ref=source, dst_ref=rowbufs[c].at[place], send_sem=ss.at[c, s], recv_sem=rr.at[c, s],
            device_id={"ctx": target}, device_id_type=MESH,
        )

    def each_hop(c, right, s, act):
        pos = z if right else last - z

        @pl.when((pos >= s) & (pos < last - 1))
        def _():
            act(hop(c, right, s, nb))

        @pl.when(pos == last - 1)
        def _():
            if s <= last - 1:
                act(hop(c, right, s, keep))

    def arrive(c, right, s):
        pos = z if right else last - z
        src_z = z - s - 1 if right else z + s + 1
        ss, rr = (right_s, right_r) if right else (left_s, left_r)

        def wait(count):
            place = rowbufs[c].at[pl.ds(src_z * nb, count)]
            pltpu.make_async_remote_copy(
                src_ref=place, dst_ref=place, send_sem=ss.at[c, s], recv_sem=rr.at[c, s],
                device_id={"ctx": peer}, device_id_type=MESH,
            ).wait_recv()

        @pl.when((pos >= s + 1) & (pos < last))
        def _():
            wait(nb)

        @pl.when(pos == last)
        def _():
            wait(keep)

    def halo_copy(c, up):
        block = nb - 1 if up else 0
        i = 0 if up else 1
        return pltpu.make_async_remote_copy(
            src_ref=kv_ref.at[:, block, :, cols(c)], dst_ref=halo.at[c, i],
            send_sem=halo_s.at[c, i], recv_sem=halo_r.at[c, i],
            device_id={"ctx": me + 1 if up else me - 1}, device_id_type=MESH,
        )

    def y_copy(c):
        return pltpu.make_async_remote_copy(
            src_ref=ysend.at[c % 2], dst_ref=ybufs[c], send_sem=y_s.at[c], recv_sem=y_r.at[c],
            device_id={"ctx": peer}, device_id_type=MESH,
        )

    def gl_copy(c, right):
        return pltpu.make_async_remote_copy(
            src_ref=ysend.at[c % 2, pl.ds(ny_slots, nglob)], dst_ref=glbuf.at[c],
            send_sem=gl_s.at[c], recv_sem=gl_r.at[c],
            device_id={"ctx": me + NY if right else me - NY}, device_id_type=MESH,
        )

    def each_gl(c, act):
        @pl.when(z == last - 1)
        def _():
            act(gl_copy(c, True))

        @pl.when(z == 1)
        def _():
            act(gl_copy(c, False))

    def own_left_sent(c):
        each_hop(c, False, 0, lambda copy: copy.wait_send())

    def begin(c):
        if c >= 3:
            own_left_sent(c - 3)
        for i in range(nb):
            rowbufs[c][z * nb + i] = kv_ref[:, tab[o_right + i], :, cols(c)]
            left_order[c % 3, i] = kv_ref[:, tab[o_left + i], :, cols(c)]
        each_hop(c, True, 0, lambda copy: copy.start())
        each_hop(c, False, 0, lambda copy: copy.start())

        @pl.when(me < nctx - 1)
        def _():
            halo_copy(c, True).start()

        @pl.when(me > 0)
        def _():
            halo_copy(c, False).start()

        @pl.when(me == 0)
        def _():
            halo[c, 0] = jnp.zeros(halo.shape[2:], halo.dtype)

        @pl.when(me == nctx - 1)
        def _():
            halo[c, 1] = jnp.zeros(halo.shape[2:], halo.dtype)

    def relay(c, s):
        arrive(c, True, s - 1)
        arrive(c, False, s - 1)
        if s < last:
            each_hop(c, True, s, lambda copy: copy.start())
            each_hop(c, False, s, lambda copy: copy.start())

    def free_across(c):
        if c >= 2:
            y_copy(c - 2).wait_send()
            each_gl(c - 2, lambda copy: copy.wait_send())

    def across(c, inner):
        pool = pools[c % 2]
        pool[: NZ * nb] = rowbufs[c][...]
        if not inner:
            gl_copy(c, True).wait_recv()
            pool[NZ * nb + ny_slots + nglob :] = glbuf[c]
        for g in range(nglob):
            ysend[c % 2, ny_slots + g] = pool[tab[o_g + g]]
        if inner:
            each_gl(c, lambda copy: copy.start())
        for i in range(ny_slots):
            ysend[c % 2, i] = pool[tab[o_y + i]]
        y_copy(c).start()

    def compute(c):
        y_copy(c).wait_recv()
        pool = pools[c % 2]
        pool[NZ * nb : NZ * nb + ny_slots + nglob] = ybufs[c][...]

        @pl.when(me > 0)
        def _():
            halo_copy(c, True).wait_recv()

        @pl.when(me < nctx - 1)
        def _():
            halo_copy(c, False).wait_recv()

        def body(b, carry):
            def own(i):
                return kv_ref[:, i, :, cols(c)]

            got = [
                lax.select(b == 0, halo[c, 0], own(jnp.maximum(b - 1, 0))),
                own(b),
                lax.select(b == nb - 1, halo[c, 1], own(jnp.minimum(b + 1, nb - 1))),
            ]
            for g in range(nglob):
                got.append(pool[tab[o_gl + g]])
            for r in range(rand):
                got.append(pool[tab[o_r + b * rand + r]])
            biases = [None] * len(got)
            biases[0] = jnp.where((b == 0) & (me == 0), NEG, 0.0).astype(jnp.float32)
            biases[2] = jnp.where((b == nb - 1) & (me == nctx - 1), NEG, 0.0).astype(jnp.float32)
            rows = pl.ds(pl.multiple_of(b * BS, BS), BS)
            t = t_ref[rows, cols(c)]
            image = attend(q_ref[rows, cols(c)], t, [x[0] for x in got], [x[1] for x in got], biases)
            out_ref[rows, cols(c)] = image
            sum_ref[0] += fold(t * image)
            sum_ref[1] += fold(image * image)
            sum_ref[2] += fold(t * t)
            return carry

        lax.fori_loop(0, nb, body, 0, unroll=2)

    pl.semaphore_wait(barrier, nctx - 1 + nhead - 1)
    sum_ref[...] = jnp.zeros_like(sum_ref)
    begin(0)
    if heads > 1:
        begin(1)
    relay(0, 1)
    inner = (z > 0) & (z < last)
    outer = (z == 0) | (z == last)
    for c in range(heads):
        relay(c, 2)
        free_across(c)

        @pl.when(inner)
        def _():
            across(c, True)

        if c + 1 < heads:
            relay(c + 1, 1)
        if c + 2 < heads:
            begin(c + 2)
        if c >= 1:
            compute(c - 1)
        relay(c, 3)

        @pl.when(outer)
        def _():
            across(c, False)

    compute(heads - 1)

    def share(buf, axis, mine, count, base):
        buf[mine] = sum_ref[...]
        copies = []
        for o in range(1, count):
            copy = pltpu.make_async_remote_copy(
                src_ref=buf.at[mine], dst_ref=buf.at[mine],
                send_sem=red_s.at[base + o - 1], recv_sem=red_r.at[base + o - 1],
                device_id={axis: lax.rem(mine + o, count)}, device_id_type=MESH,
            )
            copy.start()
            copies.append(copy)
        for o in range(1, count):
            place = buf.at[lax.rem(mine + count - o, count)]
            pltpu.make_async_remote_copy(
                src_ref=place, dst_ref=place,
                send_sem=red_s.at[base + o - 1], recv_sem=red_r.at[base + o - 1],
                device_id={axis: lax.rem(mine + o, count)}, device_id_type=MESH,
            ).wait_recv()
        total = buf[0]
        for i in range(1, count):
            total = total + buf[i]
        sum_ref[...] = total
        for copy in copies:
            copy.wait_send()

    share(red1, "head", hd, nhead, 0)
    share(red2, "ctx", me, nctx, nhead - 1)

    def whole(i):
        return jnp.sum(jnp.sum(sum_ref[i], axis=0, keepdims=True), axis=1, keepdims=True)

    count = float(nb * BS * heads * HD * nctx * nhead)
    cross, image_sum, vector = whole(0), whole(1), whole(2)
    alpha = cross / count
    square = image_sum - 2.0 * alpha * cross + alpha * alpha * vector
    beta = jnp.sqrt(square / count + 1e-06)
    coef_ref[0:1] = jnp.broadcast_to(alpha, (1, HD))
    coef_ref[1:2] = jnp.broadcast_to(beta, (1, HD))
    inverse_beta = 1.0 / beta

    def scale(b, carry):
        rows = pl.ds(pl.multiple_of(b * 16, 16), 16)
        out_ref[rows, :] = (out_ref[rows, :] - alpha * t_ref[rows, :]) * inverse_beta
        return carry

    lax.fori_loop(0, nb * BS // 16, scale, 0)

    for c in range(heads):
        for s in range(last):
            each_hop(c, True, s, lambda copy: copy.wait_send())
            if s > 0 or c >= heads - 3:
                each_hop(c, False, s, lambda copy: copy.wait_send())

        @pl.when(me < nctx - 1)
        def _():
            halo_copy(c, True).wait_send()

        @pl.when(me > 0)
        def _():
            halo_copy(c, False).wait_send()

        if c >= heads - 2:
            y_copy(c).wait_send()
            each_gl(c, lambda copy: copy.wait_send())


def line_tables(rand_blocks, global_ids, nb, me, cap, keep):
    n = NZ * NY
    z, y = me // NY, me % NY
    requests = rand_blocks.reshape(n, -1)
    wanted = (requests[:, None, :] == jnp.arange(n * nb, dtype=jnp.int32)[None, :, None]).any(axis=2)
    layer = wanted.reshape(NZ, NY, n * nb).any(axis=1)

    def order(need):
        need = need.reshape(n, nb).astype(jnp.int32)
        first = jnp.cumsum(need, axis=1)
        rest = jnp.cumsum(1 - need, axis=1)
        rank = jnp.where(need == 1, first - 1, first[:, -1:] + rest - 1)
        return rank

    rank_r = order(layer[NZ - 1])
    rank_l = order(layer[0])
    ids = jnp.arange(nb, dtype=jnp.int32)

    def inverse(rank):
        mine = lax.dynamic_index_in_dim(rank, me, 0, keepdims=False)
        return jnp.sum(jnp.where(mine[None, :] == ids[:, None], ids[None, :], 0), axis=1)

    src_z = jnp.arange(n, dtype=jnp.int32) // NY
    rank = jnp.where((src_z <= z)[:, None], rank_r, rank_l)
    place = (src_z[:, None] * nb + rank).reshape(-1)

    def lookup(blocks):
        hit = blocks[:, None] == jnp.arange(n * nb, dtype=jnp.int32)[None, :]
        return jnp.sum(jnp.where(hit, place[None, :], 0), axis=1)

    def ranks(req):
        source = req // nb
        total = req.shape[0]
        before = jnp.arange(total)[:, None] > jnp.arange(total)[None, :]
        return jnp.sum((before & (source[:, None] == source[None, :])).astype(jnp.int32), axis=1)

    own = lax.dynamic_index_in_dim(requests, me, 0, keepdims=False)
    other = lax.dynamic_index_in_dim(requests, z * NY + (NY - 1 - y), 0, keepdims=False)
    other_src = other // nb
    other_slot = jnp.where(other_src % NY == y, (other_src // NY) * cap + ranks(other), -1)
    slot = jnp.arange(NZ * cap, dtype=jnp.int32)
    y_src = jnp.sum(jnp.where(other_slot[None, :] == slot[:, None], lookup(other)[None, :], 0), axis=1)
    g_owner = global_ids // nb
    g_ids = jnp.arange(global_ids.shape[0], dtype=jnp.int32)
    far = ((z == 0) | (z == NZ - 1)) & (g_owner // NY != z)
    y_base = NZ * nb
    g_base = y_base + NZ * cap
    g_src = jnp.where(far, g_base + g_ids.shape[0] + g_ids, lookup(global_ids))
    g_all = jnp.where(g_owner % NY == y, g_src, g_base + g_ids)
    own_src = own // nb
    r_all = jnp.where(own_src % NY == y, lookup(own), y_base + (own_src // NY) * cap + ranks(own))
    parts = [inverse(rank_r), inverse(rank_l), y_src, g_src, g_all, r_all]
    return jnp.concatenate([p.astype(jnp.int32) for p in parts])


def line_local(queries, key_value, lanczos_vec, rand_blocks, global_ids):
    rows, cols = queries.shape
    nb = rows // BS
    heads = cols // HD
    n = lax.axis_size("ctx")
    nhead = lax.axis_size("head")
    me = lax.axis_index("ctx")
    rand = rand_blocks.shape[1]
    nglob = global_ids.shape[0]
    cap = (nb * rand + n - 1) // n
    keep = min(nb, NY * cap)
    tab = line_tables(rand_blocks, global_ids, nb, me, cap, keep)
    slots = NZ * cap + nglob
    dims = (nb, heads, rand, nglob, cap, keep, n, nhead)
    unit = (2, BS, HD)
    vmem = pl.BlockSpec(memory_space=pltpu.VMEM)
    sem = pltpu.SemaphoreType.DMA
    next_vec, coefs = pl.pallas_call(
        functools.partial(line_kernel, dims),
        in_specs=[pl.BlockSpec(memory_space=pltpu.SMEM), vmem, vmem, vmem],
        out_specs=[vmem, vmem],
        out_shape=[
            jax.ShapeDtypeStruct((rows, cols), jnp.float32),
            jax.ShapeDtypeStruct((2, HD), jnp.float32),
        ],
        scratch_shapes=[pltpu.VMEM((NZ * nb,) + unit, jnp.bfloat16)] * heads
        + [pltpu.VMEM((slots,) + unit, jnp.bfloat16)] * heads
        + [
            pltpu.VMEM((NZ * nb + slots + nglob,) + unit, jnp.bfloat16),
            pltpu.VMEM((NZ * nb + slots + nglob,) + unit, jnp.bfloat16),
            pltpu.VMEM((3, 8, HD), jnp.float32),
            pltpu.VMEM((2, slots) + unit, jnp.bfloat16),
            pltpu.VMEM((3, nb) + unit, jnp.bfloat16),
            pltpu.VMEM((heads, nglob) + unit, jnp.bfloat16),
            pltpu.VMEM((heads, 2) + unit, jnp.bfloat16),
            pltpu.VMEM((nhead, 3, 8, HD), jnp.float32),
            pltpu.VMEM((n, 3, 8, HD), jnp.float32),
            sem((heads, NZ)), sem((heads, NZ)), sem((heads, NZ)), sem((heads, NZ)),
            sem((heads,)), sem((heads,)), sem((heads,)), sem((heads,)),
            sem((heads, 2)), sem((heads, 2)),
            sem((n + nhead,)), sem((n + nhead,)),
        ],
        compiler_params=pltpu.CompilerParams(
            collective_id=0, has_side_effects=True, vmem_limit_bytes=VMEM_LIMIT
        ),
    )(tab, queries, lanczos_vec, key_value.reshape(2, nb, BS, cols))
    return next_vec, coefs[:, 0]


def solution(mesh):
    placed = (P("ctx", "head"), P(None, "ctx", "head"), P("ctx", "head"), P(), P())
    body = line_local if mesh.shape["ctx"] == NZ * NY else local
    return jax.shard_map(
        body, mesh=mesh, in_specs=placed, out_specs=(P("ctx", "head"), P()), check_vma=False
    )
```

```python
import functools

import jax
import jax.numpy as jnp
from jax import lax
from jax.experimental import pallas as pl
from jax.experimental.pallas import tpu as pltpu
from jax.sharding import PartitionSpec as P

HD = 128
BS = 128
SCALE = HD ** (-0.5)
LOG2E = 1.4426950408889634
NEG = float("-inf")
CHUNKS = 4
VMEM_LIMIT = 56 * 1024 * 1024
NZ = 4
NY = 2
MESH = pl.DeviceIdType.MESH


def attend(q, t, keys, vals, biases):
    k = jnp.concatenate(keys, axis=0)
    v = jnp.concatenate(vals, axis=0)
    nt = (((1,), (1,)), ((), ()))
    nn = (((1,), (0,)), ((), ()))
    both = lax.dot_general(
        jnp.concatenate([q, t.astype(jnp.bfloat16)], axis=0), k, nt,
        preferred_element_type=jnp.float32,
    )
    s = both[:BS]
    ds = both[BS:]
    parts = []
    for i in range(len(keys)):
        part = s[:, i * BS : (i + 1) * BS]
        parts.append(part if biases[i] is None else part + biases[i])
    s = jnp.concatenate(parts, axis=1)
    top = jnp.max(s, axis=1, keepdims=True)
    w = jnp.exp2((s - top) * (SCALE * LOG2E))
    inv = 1.0 / jnp.sum(w, axis=1, keepdims=True)
    p = w * inv
    center = jnp.sum(p * ds, axis=1, keepdims=True)
    g = ((p * SCALE) * (ds - center)).astype(jnp.bfloat16)
    dout = lax.dot_general(g, v, nn, preferred_element_type=jnp.float32).astype(jnp.bfloat16)
    dp = lax.dot_general(dout, v, nt, preferred_element_type=jnp.float32)
    center2 = jnp.sum(p * dp, axis=1, keepdims=True)
    g2 = (p * (dp - center2)).astype(jnp.bfloat16)
    return lax.dot_general(g2, k, nn, preferred_element_type=jnp.float32) * SCALE


def fold(x):
    return jnp.sum(x.reshape(BS // 8, 8, HD), axis=0)


def attend_kernel(nblocks, rand, slots, edge, q_ref, t_ref, kv_ref, lo_ref, hi_ref, gl_ref, in_ref, *rest):
    out_ref, sum_ref = rest[-2:]
    h = pl.program_id(0)

    @pl.when(h == 0)
    def _():
        sum_ref[...] = jnp.zeros_like(sum_ref)

    def block(b):
        rows = pl.ds(b * BS, BS)

        def listed(i):
            got = []
            if b == 0:
                got.append(lo_ref[i])
            else:
                got.append(kv_ref[i, (b - 1) * BS : b * BS, :])
            got.append(kv_ref[i, b * BS : (b + 1) * BS, :])
            if b == nblocks - 1:
                got.append(hi_ref[i])
            else:
                got.append(kv_ref[i, (b + 1) * BS : (b + 2) * BS, :])
            for g in range(gl_ref.shape[1] // BS):
                got.append(gl_ref[i, g * BS : (g + 1) * BS, :])
            for r in range(rand):
                got.append(in_ref[slots[b * rand + r], i])
            return got

        keys, vals = listed(0), listed(1)
        biases = [None] * len(keys)
        if b == 0:
            biases[0] = jnp.where(edge[0] > 0, NEG, 0.0).astype(jnp.float32)
        if b == nblocks - 1:
            biases[2] = jnp.where(edge[1] > 0, NEG, 0.0).astype(jnp.float32)
        t = t_ref[rows, :]
        image = attend(q_ref[rows, :], t, keys, vals, biases)
        out_ref[rows, :] = image
        sum_ref[0] += fold(t * image)
        sum_ref[1] += fold(image * image)
        sum_ref[2] += fold(t * t)

    for b in range(nblocks):
        block(b)


def attend_chunk(c, heads, queries, vec, key_value, lo, hi, glob, incoming, slots, edge, product):
    rows, width = queries.shape
    nblocks = rows // BS
    nslots = incoming.shape[0]
    rand = slots.shape[0] // nblocks
    first = c * heads
    col = lambda h, *_: (0, first + h)
    col3 = lambda h, *_: (0, 0, first + h)
    in_specs = [
        pl.BlockSpec((rows, HD), col),
        pl.BlockSpec((rows, HD), col),
        pl.BlockSpec((2, rows, HD), col3),
        pl.BlockSpec((2, BS, HD), col3),
        pl.BlockSpec((2, BS, HD), col3),
        pl.BlockSpec((2, glob.shape[1], HD), col3),
        pl.BlockSpec((nslots, 2, BS, HD), lambda h, *_: (0, 0, 0, h)),
    ]
    args = [slots, edge, queries, vec, key_value, lo, hi, glob, incoming]
    aliases = {}
    if product is not None:
        in_specs.append(pl.BlockSpec(memory_space=pl.ANY))
        aliases = {len(args): 0}
        args.append(product)
    return pl.pallas_call(
        functools.partial(attend_kernel, nblocks, rand),
        grid_spec=pltpu.PrefetchScalarGridSpec(
            num_scalar_prefetch=2,
            grid=(heads,),
            in_specs=in_specs,
            out_specs=[
                pl.BlockSpec((rows, HD), col),
                pl.BlockSpec((3, 8, HD), lambda h, *_: (0, 0, 0)),
            ],
        ),
        out_shape=[
            jax.ShapeDtypeStruct((rows, width), jnp.float32),
            jax.ShapeDtypeStruct((3, 8, HD), jnp.float32),
        ],
        input_output_aliases=aliases,
        compiler_params=pltpu.CompilerParams(vmem_limit_bytes=VMEM_LIMIT),
        cost_estimate=pl.CostEstimate(
            flops=heads * nblocks * 5 * 2 * BS * HD * 8 * BS * 4, bytes_accessed=heads * 8 * 2**20, transcendentals=0
        ),
    )(*args)


def pick_kernel(chosen, kv_ref, *outs):
    width = outs[0].shape[-1]
    for c, out in enumerate(outs):
        out[0] = kv_ref[:, :, c * width : (c + 1) * width]


def pick_blocks(key_value, chosen):
    count = chosen.shape[0]
    cols = key_value.shape[2]
    width = cols // CHUNKS
    return pl.pallas_call(
        pick_kernel,
        grid_spec=pltpu.PrefetchScalarGridSpec(
            num_scalar_prefetch=1,
            grid=(count,),
            in_specs=[pl.BlockSpec((2, BS, cols), lambda i, chosen: (0, chosen[i], 0))],
            out_specs=[pl.BlockSpec((1, 2, BS, width), lambda i, chosen: (i, 0, 0, 0))] * CHUNKS,
        ),
        out_shape=[jax.ShapeDtypeStruct((count, 2, BS, width), key_value.dtype)] * CHUNKS,
    )(chosen, key_value)


def from_root(block, axis, holder):
    block = jnp.where(lax.axis_index(axis) == holder, block, jnp.zeros_like(block))
    return lax.psum(block, axis)


def request_tables(rand_blocks, nblocks, ctx_count, ctx_index, capacity):
    requests = rand_blocks.reshape(ctx_count, -1)
    sources = requests // nblocks
    inside = requests % nblocks
    mine = (sources == ctx_index).astype(jnp.int32)
    earlier = jnp.cumsum(mine, axis=1) - mine
    slot_ids = jnp.arange(capacity, dtype=jnp.int32)
    matched = (mine[:, :, None] == 1) & (earlier[:, :, None] == slot_ids[None, None, :])
    chosen = jnp.sum(jnp.where(matched, inside[:, :, None], 0), axis=1).reshape(-1)
    own = lax.dynamic_index_in_dim(sources, ctx_index, 0, keepdims=False)
    total = own.shape[0]
    before = jnp.arange(total)[:, None] > jnp.arange(total)[None, :]
    same = own[:, None] == own[None, :]
    rank = jnp.sum((before & same).astype(jnp.int32), axis=1)
    return chosen, own * capacity + rank


def local(queries, key_value, lanczos_vec, rand_blocks, global_ids):
    rows, cols = queries.shape
    nblocks = rows // BS
    n = lax.axis_size("ctx")
    me = lax.axis_index("ctx")
    rand = rand_blocks.shape[1]
    capacity = (nblocks * rand + n - 1) // n
    chosen, slots = request_tables(rand_blocks, nblocks, n, me, capacity)
    outgoing = pick_blocks(key_value, chosen)
    incoming = [lax.all_to_all(part, "ctx", split_axis=0, concat_axis=0, tiled=True) for part in outgoing]
    lo = lax.ppermute(key_value[:, rows - BS :], "ctx", [(i, i + 1) for i in range(n - 1)])
    hi = lax.ppermute(key_value[:, :BS], "ctx", [(i + 1, i) for i in range(n - 1)])
    pieces = []
    for g in range(global_ids.shape[0]):
        piece = lax.dynamic_slice_in_dim(key_value, global_ids[g] % nblocks * BS, BS, 1)
        pieces.append(from_root(piece, "ctx", global_ids[g] // nblocks))
    glob = jnp.concatenate(pieces, axis=1)
    edge = jnp.stack([me == 0, me == n - 1]).astype(jnp.int32)
    product = None
    sums = 0.0
    heads = cols // HD // CHUNKS
    for c in range(CHUNKS):
        product, part = attend_chunk(
            c, heads, queries, lanczos_vec, key_value, lo, hi, glob, incoming[c], slots, edge, product
        )
        sums = sums + part
    totals = lax.psum(jnp.sum(sums, axis=(1, 2)), ("ctx", "head"))
    return finish(product, lanczos_vec, totals, float(rows * cols * n * lax.axis_size("head")))


def finish(product, vec, totals, count):
    cross, image, vector = totals[0], totals[1], totals[2]
    alpha = cross / count
    square = image - 2.0 * alpha * cross + alpha * alpha * vector
    beta = jnp.sqrt(square / count + 1e-06)
    return (product - alpha * vec) / beta, jnp.stack([alpha, beta])


def line_kernel(dims, tab, q_ref, t_ref, kv_ref, out_ref, coef_ref, *scratch):
    nb, heads, rand, nglob, cap, keep, nctx, nhead = dims
    rowbufs = scratch[:heads]
    ybufs = scratch[heads : 2 * heads]
    fars = scratch[2 * heads : 3 * heads]
    (pool_a, pool_b, sum_ref, ysend, left_order, glbuf, halo, red1, red2, right_s, right_r, left_s, left_r,
     y_s, y_r, yf_s, yf_r, yg_s, yg_r, gl_s, gl_r, halo_s, halo_r, red_s, red_r) = scratch[3 * heads :]
    pools = (pool_a, pool_b)
    ny_slots = NZ * cap
    o_right, o_left = 0, nb
    o_y = 2 * nb
    o_g = o_y + ny_slots
    o_gl = o_g + nglob
    o_r = o_gl + nglob
    me = lax.axis_index("ctx")
    hd = lax.axis_index("head")
    z = me // NY
    y = me % NY
    peer = z * NY + (NY - 1 - y)
    last = NZ - 1

    barrier = pltpu.get_barrier_semaphore()
    for o in range(1, nctx):
        pl.semaphore_signal(barrier, inc=1, device_id={"ctx": lax.rem(me + o, nctx)}, device_id_type=MESH)
    for o in range(1, nhead):
        pl.semaphore_signal(barrier, inc=1, device_id={"head": lax.rem(hd + o, nhead)}, device_id_type=MESH)

    def cols(c):
        return slice(c * HD, (c + 1) * HD)

    def hop(c, right, s, count):
        pos_z = z - s if right else z + s
        place = pl.ds(pos_z * nb, count)
        target = me + NY if right else me - NY
        if s == 0 and not right:
            source = left_order.at[c % 3, pl.ds(0, count)]
        else:
            source = rowbufs[c].at[place]
        ss, rr = (right_s, right_r) if right else (left_s, left_r)
        return pltpu.make_async_remote_copy(
            src_ref=source, dst_ref=fars[c] if s == last - 1 else rowbufs[c].at[place], send_sem=ss.at[c, s], recv_sem=rr.at[c, s],
            device_id={"ctx": target}, device_id_type=MESH,
        )

    def each_hop(c, right, s, act):
        pos = z if right else last - z

        if s < last - 1:

            @pl.when((pos >= s) & (pos < last - 1))
            def _():
                act(hop(c, right, s, nb))

        @pl.when(pos == last - 1)
        def _():
            if s <= last - 1:
                act(hop(c, right, s, keep))

    def arrive(c, right, s):
        pos = z if right else last - z
        src_z = z - s - 1 if right else z + s + 1
        ss, rr = (right_s, right_r) if right else (left_s, left_r)

        def wait(count):
            place = fars[c] if s == last - 1 else rowbufs[c].at[pl.ds(src_z * nb, count)]
            pltpu.make_async_remote_copy(
                src_ref=place, dst_ref=place, send_sem=ss.at[c, s], recv_sem=rr.at[c, s],
                device_id={"ctx": peer}, device_id_type=MESH,
            ).wait_recv()

        if s < last - 1:

            @pl.when((pos >= s + 1) & (pos < last))
            def _():
                wait(nb)

        @pl.when(pos == last)
        def _():
            wait(keep)

    def halo_copy(c, up):
        block = nb - 1 if up else 0
        i = 0 if up else 1
        return pltpu.make_async_remote_copy(
            src_ref=kv_ref.at[:, block, :, cols(c)], dst_ref=halo.at[c, i],
            send_sem=halo_s.at[c, i], recv_sem=halo_r.at[c, i],
            device_id={"ctx": me + 1 if up else me - 1}, device_id_type=MESH,
        )

    def y_copy(c):
        return pltpu.make_async_remote_copy(
            src_ref=ysend.at[c % 2], dst_ref=ybufs[c], send_sem=y_s.at[c], recv_sem=y_r.at[c],
            device_id={"ctx": peer}, device_id_type=MESH,
        )

    def gl_copy(c, right):
        return pltpu.make_async_remote_copy(
            src_ref=ysend.at[c % 2, pl.ds(ny_slots, nglob)], dst_ref=glbuf.at[c],
            send_sem=gl_s.at[c], recv_sem=gl_r.at[c],
            device_id={"ctx": me + NY if right else me - NY}, device_id_type=MESH,
        )

    def each_gl(c, act):
        @pl.when(z == last - 1)
        def _():
            act(gl_copy(c, True))

        @pl.when(z == 1)
        def _():
            act(gl_copy(c, False))

    def own_left_sent(c):
        each_hop(c, False, 0, lambda copy: copy.wait_send())

    def begin(c):
        if c >= 3:
            own_left_sent(c - 3)
        for i in range(nb):
            rowbufs[c][z * nb + i] = kv_ref[:, tab[o_right + i], :, cols(c)]
            left_order[c % 3, i] = kv_ref[:, tab[o_left + i], :, cols(c)]
        each_hop(c, True, 0, lambda copy: copy.start())
        each_hop(c, False, 0, lambda copy: copy.start())

        @pl.when(me < nctx - 1)
        def _():
            halo_copy(c, True).start()

        @pl.when(me > 0)
        def _():
            halo_copy(c, False).start()

        @pl.when(me == 0)
        def _():
            halo[c, 0] = jnp.zeros(halo.shape[2:], halo.dtype)

        @pl.when(me == nctx - 1)
        def _():
            halo[c, 1] = jnp.zeros(halo.shape[2:], halo.dtype)

    def relay(c, s):
        arrive(c, True, s - 1)
        arrive(c, False, s - 1)
        if s < last:
            each_hop(c, True, s, lambda copy: copy.start())
            each_hop(c, False, s, lambda copy: copy.start())

    far_z = jnp.where(z == 0, last, 0)
    near_slot = jnp.where(z == 0, 0, cap)
    inner = (z > 0) & (z < last)
    outer = (z == 0) | (z == last)

    def y_part(c, start, count, send, recv):
        return pltpu.make_async_remote_copy(
            src_ref=ysend.at[c % 2, pl.ds(start, count)], dst_ref=ybufs[c].at[pl.ds(start, count)],
            send_sem=send.at[c], recv_sem=recv.at[c],
            device_id={"ctx": peer}, device_id_type=MESH,
        )

    def y_near(c):
        return y_part(c, near_slot, ny_slots - cap, y_s, y_r)

    def y_far(c):
        return y_part(c, far_z * cap, cap, yf_s, yf_r)

    def y_glob(c):
        return y_part(c, ny_slots, nglob, yg_s, yg_r)

    def each_y(c, act):
        @pl.when(inner)
        def _():
            act(y_copy(c))

        @pl.when(outer)
        def _():
            act(y_near(c))
            act(y_far(c))
            act(y_glob(c))

    def free_across(c):
        if c >= 2:
            each_y(c - 2, lambda copy: copy.wait_send())
            each_gl(c - 2, lambda copy: copy.wait_send())

    def across(c):
        pool = pools[c % 2]
        pool[: NZ * nb] = rowbufs[c][...]
        for i in range(ny_slots):
            ysend[c % 2, i] = pool[tab[o_y + i]]

        @pl.when(inner)
        def _():
            for g in range(nglob):
                ysend[c % 2, ny_slots + g] = pool[tab[o_g + g]]
            each_gl(c, lambda copy: copy.start())
            y_copy(c).start()

        @pl.when(outer)
        def _():
            y_near(c).start()

    def across_late(c):
        pool = pools[c % 2]

        @pl.when(outer)
        def _():
            pool[pl.ds(far_z * nb, keep)] = fars[c][...]
            for k in range(cap):
                ysend[c % 2, far_z * cap + k] = pool[tab[o_y + far_z * cap + k]]
            y_far(c).start()
            gl_copy(c, True).wait_recv()
            pool[NZ * nb + ny_slots + nglob :] = glbuf[c]
            for g in range(nglob):
                ysend[c % 2, ny_slots + g] = pool[tab[o_g + g]]
            y_glob(c).start()

    def compute(c):
        each_y(c, lambda copy: copy.wait_recv())
        pool = pools[c % 2]
        pool[NZ * nb : NZ * nb + ny_slots + nglob] = ybufs[c][...]

        @pl.when(me > 0)
        def _():
            halo_copy(c, True).wait_recv()

        @pl.when(me < nctx - 1)
        def _():
            halo_copy(c, False).wait_recv()

        def body(b, carry):
            def own(i):
                return kv_ref[:, i, :, cols(c)]

            got = [
                lax.select(b == 0, halo[c, 0], own(jnp.maximum(b - 1, 0))),
                own(b),
                lax.select(b == nb - 1, halo[c, 1], own(jnp.minimum(b + 1, nb - 1))),
            ]
            for g in range(nglob):
                got.append(pool[tab[o_gl + g]])
            for r in range(rand):
                got.append(pool[tab[o_r + b * rand + r]])
            biases = [None] * len(got)
            biases[0] = jnp.where((b == 0) & (me == 0), NEG, 0.0).astype(jnp.float32)
            biases[2] = jnp.where((b == nb - 1) & (me == nctx - 1), NEG, 0.0).astype(jnp.float32)
            rows = pl.ds(pl.multiple_of(b * BS, BS), BS)
            t = t_ref[rows, cols(c)]
            image = attend(q_ref[rows, cols(c)], t, [x[0] for x in got], [x[1] for x in got], biases)
            out_ref[rows, cols(c)] = image
            sum_ref[0] += fold(t * image)
            sum_ref[1] += fold(image * image)
            sum_ref[2] += fold(t * t)
            return carry

        lax.fori_loop(0, nb, body, 0)

    pl.semaphore_wait(barrier, nctx - 1 + nhead - 1)
    sum_ref[...] = jnp.zeros_like(sum_ref)
    begin(0)
    if heads > 1:
        begin(1)
    relay(0, 1)
    for c in range(heads):
        relay(c, 2)
        free_across(c)
        across(c)
        if c + 1 < heads:
            relay(c + 1, 1)
        if c + 2 < heads:
            begin(c + 2)
        if c >= 1:
            compute(c - 1)
        relay(c, 3)
        across_late(c)

    compute(heads - 1)

    def share(buf, axis, mine, count, base):
        buf[mine] = sum_ref[...]
        copies = []
        for o in range(1, count):
            copy = pltpu.make_async_remote_copy(
                src_ref=buf.at[mine], dst_ref=buf.at[mine],
                send_sem=red_s.at[base + o - 1], recv_sem=red_r.at[base + o - 1],
                device_id={axis: lax.rem(mine + o, count)}, device_id_type=MESH,
            )
            copy.start()
            copies.append(copy)
        for o in range(1, count):
            place = buf.at[lax.rem(mine + count - o, count)]
            pltpu.make_async_remote_copy(
                src_ref=place, dst_ref=place,
                send_sem=red_s.at[base + o - 1], recv_sem=red_r.at[base + o - 1],
                device_id={axis: lax.rem(mine + o, count)}, device_id_type=MESH,
            ).wait_recv()
        total = buf[0]
        for i in range(1, count):
            total = total + buf[i]
        sum_ref[...] = total
        for copy in copies:
            copy.wait_send()

    share(red1, "head", hd, nhead, 0)
    share(red2, "ctx", me, nctx, nhead - 1)

    def whole(i):
        return jnp.sum(jnp.sum(sum_ref[i], axis=0, keepdims=True), axis=1, keepdims=True)

    count = float(nb * BS * heads * HD * nctx * nhead)
    cross, image_sum, vector = whole(0), whole(1), whole(2)
    alpha = cross / count
    square = image_sum - 2.0 * alpha * cross + alpha * alpha * vector
    beta = jnp.sqrt(square / count + 1e-06)
    coef_ref[0:1] = jnp.broadcast_to(alpha, (1, HD))
    coef_ref[1:2] = jnp.broadcast_to(beta, (1, HD))
    inverse_beta = 1.0 / beta

    def scale(b, carry):
        rows = pl.ds(pl.multiple_of(b * 16, 16), 16)
        out_ref[rows, :] = (out_ref[rows, :] - alpha * t_ref[rows, :]) * inverse_beta
        return carry

    lax.fori_loop(0, nb * BS // 16, scale, 0)

    for c in range(heads):
        for s in range(last):
            each_hop(c, True, s, lambda copy: copy.wait_send())
            if s > 0 or c >= heads - 3:
                each_hop(c, False, s, lambda copy: copy.wait_send())

        @pl.when(me < nctx - 1)
        def _():
            halo_copy(c, True).wait_send()

        @pl.when(me > 0)
        def _():
            halo_copy(c, False).wait_send()

        if c >= heads - 2:
            each_y(c, lambda copy: copy.wait_send())
            each_gl(c, lambda copy: copy.wait_send())


def line_tables(rand_blocks, global_ids, nb, me, cap, keep):
    n = NZ * NY
    z, y = me // NY, me % NY
    requests = rand_blocks.reshape(n, -1)
    wanted = (requests[:, None, :] == jnp.arange(n * nb, dtype=jnp.int32)[None, :, None]).any(axis=2)
    layer = wanted.reshape(NZ, NY, n * nb).any(axis=1)

    def order(need):
        need = need.reshape(n, nb).astype(jnp.int32)
        first = jnp.cumsum(need, axis=1)
        rest = jnp.cumsum(1 - need, axis=1)
        rank = jnp.where(need == 1, first - 1, first[:, -1:] + rest - 1)
        return rank

    rank_r = order(layer[NZ - 1])
    rank_l = order(layer[0])
    ids = jnp.arange(nb, dtype=jnp.int32)

    def inverse(rank):
        mine = lax.dynamic_index_in_dim(rank, me, 0, keepdims=False)
        return jnp.sum(jnp.where(mine[None, :] == ids[:, None], ids[None, :], 0), axis=1)

    src_z = jnp.arange(n, dtype=jnp.int32) // NY
    rank = jnp.where((src_z <= z)[:, None], rank_r, rank_l)
    place = (src_z[:, None] * nb + rank).reshape(-1)

    def lookup(blocks):
        hit = blocks[:, None] == jnp.arange(n * nb, dtype=jnp.int32)[None, :]
        return jnp.sum(jnp.where(hit, place[None, :], 0), axis=1)

    def ranks(req):
        source = req // nb
        total = req.shape[0]
        before = jnp.arange(total)[:, None] > jnp.arange(total)[None, :]
        return jnp.sum((before & (source[:, None] == source[None, :])).astype(jnp.int32), axis=1)

    own = lax.dynamic_index_in_dim(requests, me, 0, keepdims=False)
    other = lax.dynamic_index_in_dim(requests, z * NY + (NY - 1 - y), 0, keepdims=False)
    other_src = other // nb
    other_slot = jnp.where(other_src % NY == y, (other_src // NY) * cap + ranks(other), -1)
    slot = jnp.arange(NZ * cap, dtype=jnp.int32)
    y_src = jnp.sum(jnp.where(other_slot[None, :] == slot[:, None], lookup(other)[None, :], 0), axis=1)
    g_owner = global_ids // nb
    g_ids = jnp.arange(global_ids.shape[0], dtype=jnp.int32)
    far = ((z == 0) | (z == NZ - 1)) & (g_owner // NY != z)
    y_base = NZ * nb
    g_base = y_base + NZ * cap
    g_src = jnp.where(far, g_base + g_ids.shape[0] + g_ids, lookup(global_ids))
    g_all = jnp.where(g_owner % NY == y, g_src, g_base + g_ids)
    own_src = own // nb
    r_all = jnp.where(own_src % NY == y, lookup(own), y_base + (own_src // NY) * cap + ranks(own))
    parts = [inverse(rank_r), inverse(rank_l), y_src, g_src, g_all, r_all]
    return jnp.concatenate([p.astype(jnp.int32) for p in parts])


def line_local(queries, key_value, lanczos_vec, rand_blocks, global_ids):
    rows, cols = queries.shape
    nb = rows // BS
    heads = cols // HD
    n = lax.axis_size("ctx")
    nhead = lax.axis_size("head")
    me = lax.axis_index("ctx")
    rand = rand_blocks.shape[1]
    nglob = global_ids.shape[0]
    cap = (nb * rand + n - 1) // n
    keep = min(nb, NY * cap)
    tab = line_tables(rand_blocks, global_ids, nb, me, cap, keep)
    slots = NZ * cap + nglob
    dims = (nb, heads, rand, nglob, cap, keep, n, nhead)
    unit = (2, BS, HD)
    vmem = pl.BlockSpec(memory_space=pltpu.VMEM)
    sem = pltpu.SemaphoreType.DMA
    next_vec, coefs = pl.pallas_call(
        functools.partial(line_kernel, dims),
        in_specs=[pl.BlockSpec(memory_space=pltpu.SMEM), vmem, vmem, vmem],
        out_specs=[vmem, vmem],
        out_shape=[
            jax.ShapeDtypeStruct((rows, cols), jnp.float32),
            jax.ShapeDtypeStruct((2, HD), jnp.float32),
        ],
        scratch_shapes=[pltpu.VMEM((NZ * nb,) + unit, jnp.bfloat16)] * heads
        + [pltpu.VMEM((slots,) + unit, jnp.bfloat16)] * heads
        + [pltpu.VMEM((keep,) + unit, jnp.bfloat16)] * heads
        + [
            pltpu.VMEM((NZ * nb + slots + nglob,) + unit, jnp.bfloat16),
            pltpu.VMEM((NZ * nb + slots + nglob,) + unit, jnp.bfloat16),
            pltpu.VMEM((3, 8, HD), jnp.float32),
            pltpu.VMEM((2, slots) + unit, jnp.bfloat16),
            pltpu.VMEM((3, nb) + unit, jnp.bfloat16),
            pltpu.VMEM((heads, nglob) + unit, jnp.bfloat16),
            pltpu.VMEM((heads, 2) + unit, jnp.bfloat16),
            pltpu.VMEM((nhead, 3, 8, HD), jnp.float32),
            pltpu.VMEM((n, 3, 8, HD), jnp.float32),
            sem((heads, NZ)), sem((heads, NZ)), sem((heads, NZ)), sem((heads, NZ)),
            sem((heads,)), sem((heads,)), sem((heads,)), sem((heads,)),
            sem((heads,)), sem((heads,)), sem((heads,)), sem((heads,)),
            sem((heads, 2)), sem((heads, 2)),
            sem((n + nhead,)), sem((n + nhead,)),
        ],
        compiler_params=pltpu.CompilerParams(
            collective_id=0, has_side_effects=True, vmem_limit_bytes=VMEM_LIMIT
        ),
    )(tab, queries, lanczos_vec, key_value.reshape(2, nb, BS, cols))
    return next_vec, coefs[:, 0]


def solution(mesh):
    placed = (P("ctx", "head"), P(None, "ctx", "head"), P("ctx", "head"), P(), P())
    body = line_local if mesh.shape["ctx"] == NZ * NY else local
    return jax.shard_map(
        body, mesh=mesh, in_specs=placed, out_specs=(P("ctx", "head"), P()), check_vma=False
    )
```
